256 devices in a mesh: dp: 4 (over y), row: 4 (over x), col: 16 (over z, core).
Axes of the slice: x: 4, y: 4, z: 8, core: 2. Of those that a mesh axis runs over, the one named last changes fastest.
Arguments:
- tokens_in: bfloat16 [1024, 12288], P(('dp', 'col'), 'row'), may hold values from -28 to 28
- out_grad: bfloat16 [1024, 49152], P('dp', 'col'), may hold values from -8 to 8
- row_state: float32 [12288], P('row'), as said below
- col_state: float32 [49152], P(('col', 'dp')), as said below
Outputs:
- update: float32 [12288, 49152], P('row', ('col', 'dp'))
- row_stats: float32 [12288], P('row')
- col_stats: float32 [49152], P(('col', 'dp'))
The draws below stay inside these ranges and needn't reach their ends.
Inputs may be any that keep to these rules, and one draw needn't show every extreme that they name: `row_state`: positive. `col_state`: positive.
All inputs are finite; a program needn't handle non-finite values.
Results may differ from the reference program's by a relative error of at most 0.0003.
Values may be sent and summed in bfloat16 or wider, within the bound.
No kernel may reach another device: no remote copies, remote signals or barrier semaphores. Data moves between devices by JAX's collectives and lax.ppermute only.
A program may use at most 64 MiB of HBM per device.

```python
import math
import jax
import jax.numpy as jnp
from jax import lax

D = 12288
F = 49152
TOKENS = 1024
N_DP = 4
N_COL = 16


def scales(key, label, length, spread):
    inner = jax.random.fold_in(key, label)
    rough = jax.random.uniform(inner, (length,), jnp.float32)
    place = (jnp.arange(length, dtype=jnp.float32) + 0.5) / length
    return jnp.exp(math.log(3.0) * (place - 0.5) + math.log(spread) * (rough - 0.5))


def levels(key, length):
    rough = jax.random.uniform(key, (length,), jnp.float32, math.log(0.1), 0.0)
    place = (jnp.arange(length, dtype=jnp.float32) + 0.5) / length
    return jnp.exp(rough - math.log(3.0) * (place - 0.5))


def falling(length, blocks, groups, ratio):
    width = length // (blocks * groups)
    group_index = jnp.arange(length, dtype=jnp.int32) // width % groups
    share = group_index.astype(jnp.float32) / max(groups - 1, 1)
    return jnp.exp(-math.log(ratio) * share)


def draw_tokens_in(key, part):
    feature = scales(key, 101, D, 10.0)
    key = jax.random.fold_in(key, 1)
    values = jnp.clip(jax.random.normal(key, (TOKENS, D), jnp.float32), -4.0, 4.0)
    return (values * feature[None, :]).astype(jnp.bfloat16)


def draw_out_grad(key, part):
    feature = scales(key, 202, F, 10.0)
    key = jax.random.fold_in(key, 2)
    values = jnp.clip(jax.random.normal(key, (TOKENS, F), jnp.float32), -4.0, 4.0)
    values = values * feature[None, :] / math.sqrt(TOKENS)
    return jnp.clip(values, -8.0, 8.0).astype(jnp.bfloat16)


def draw_row_state(key, part):
    feature = scales(key, 101, D, 10.0)
    key = jax.random.fold_in(key, 3)
    return (feature * feature * 2.6 * levels(key, D)).astype(jnp.float32)


def draw_col_state(key, part):
    feature = scales(key, 202, F, 10.0)
    tilt = falling(F, N_COL, N_DP, 6.0)
    key = jax.random.fold_in(key, 4)
    return (feature * feature * 2.6 * levels(key, F) * tilt).astype(jnp.float32)


def setup_inputs(seed: int = 0) -> dict:
    arg_keys = jax.random.split(jax.random.key(seed), 5)
    tokens_in = draw_tokens_in(jax.random.fold_in(arg_keys[4], 71), 0)
    out_grad = draw_out_grad(jax.random.fold_in(arg_keys[4], 71), 0)
    row_state = draw_row_state(jax.random.fold_in(arg_keys[4], 71), 0)
    col_state = draw_col_state(jax.random.fold_in(arg_keys[4], 71), 0)
    return dict(tokens_in=tokens_in, out_grad=out_grad, row_state=row_state, col_state=col_state)


DECAY = 0.7
CLIP = 1.0

def reference(tokens_in, out_grad, row_state, col_state):
    weight_grad = jnp.dot(tokens_in.T, out_grad, preferred_element_type=jnp.float32)
    squared = weight_grad * weight_grad
    row_stats = DECAY * row_state + (1.0 - DECAY) * (lax.optimization_barrier(jnp.sum(squared, axis=1)) / F)
    col_stats = DECAY * col_state + (1.0 - DECAY) * (lax.optimization_barrier(jnp.sum(squared, axis=0)) / D)
    row_mean = jnp.sum(row_stats) / D
    raw_update = weight_grad * lax.rsqrt(row_stats / row_mean)[:, None] * lax.rsqrt(col_stats)[None, :]
    power_mean = jnp.sum(raw_update * raw_update) / (D * F)
    clip_factor = jnp.maximum(1.0, jnp.sqrt(power_mean) / CLIP)
    return (raw_update / clip_factor, row_stats, col_stats)
```

```python
import jax
import jax.numpy as jnp
from jax import lax
from jax.sharding import Mesh, PartitionSpec as P

D = 12288
F = 49152
DECAY = 0.7
CLIP = 1.0
SIZE = {"dp": 4, "row": 4, "z": 8, "core": 2}
Z_ORDER = (0, -1, 1, -2, 2, -3, 3, 4)


def shift(x, axis, step):
    n = SIZE[axis]
    return lax.ppermute(x, axis, [(i, (i + step) % n) for i in range(n)])


def ring(x, axis):
    n = SIZE[axis]
    fwd = bwd = x
    out = [x]
    for _ in range(n // 2 - 1):
        fwd, bwd = shift(fwd, axis, 1), shift(bwd, axis, -1)
        out += [fwd, bwd]
    half = x.shape[1] // 2
    far = [shift(fwd[:, :half], axis, 1), shift(bwd[:, half:], axis, -1)]
    return out + [jnp.concatenate(far, axis=1)]


def direct(x, axis):
    return [x] + [shift(x, axis, s) for s in range(1, SIZE[axis])]


def both_cores(x):
    return jnp.concatenate([x, shift(x, "core", 1)], axis=0)


def pair_total(x, axis):
    return x + lax.ppermute(x, axis, [(i, i ^ 1) for i in range(SIZE[axis])])


def total(x, axis, step):
    return (x + shift(x, axis, 2 * step)) + (shift(x, axis, step) + shift(x, axis, -step))


def on_device(tokens_in, out_grad, row_state, col_state):
    z, core, dp = lax.axis_index("z"), lax.axis_index("core"), lax.axis_index("dp")
    g = out_grad.reshape(8, 2, 16, 3072)
    g = lax.dynamic_slice_in_dim(jnp.concatenate([g, g], axis=0), z, 8, axis=0)
    g = jnp.stack([g[r % 8] for r in Z_ORDER], axis=0)
    g = jnp.where(core == 0, g, g[:, ::-1])
    got = [
        shift(lax.dynamic_slice_in_dim(g, ((dp + s) % 4) * 768, 768, axis=3), "dp", s)
        if s else lax.dynamic_slice_in_dim(g, dp * 768, 768, axis=3)
        for s in range(4)
    ]
    b = jnp.stack(got, axis=0)
    b_first = b.transpose(2, 1, 0, 3, 4).reshape(1024, 768)
    b_second = b.transpose(2, 0, 1, 3, 4).reshape(1024, 768)

    a_first = ring(jnp.concatenate(direct(tokens_in[:, :1536], "dp"), axis=0), "z")
    a_second = direct(jnp.concatenate(ring(tokens_in[:, 1536:], "z"), axis=0), "dp")
    a_first = both_cores(jnp.concatenate(a_first, axis=0))
    a_second = both_cores(jnp.concatenate(a_second, axis=0))

    def product(a, b):
        return lax.dot_general(
            a, b, (((0,), (0,)), ((), ())), preferred_element_type=jnp.float32
        )

    grad = jnp.concatenate([product(a_first, b_first), product(a_second, b_second)], axis=0)
    squared = grad * grad
    row_part = jnp.sum(squared, axis=1)
    col_sum = total(jnp.sum(squared, axis=0), "row", 1)
    col_stats = DECAY * col_state + (1.0 - DECAY) * (col_sum / D)
    col_scale = lax.rsqrt(col_stats)
    scaled = grad * col_scale[None, :]
    parts = jnp.stack([row_part, jnp.sum(scaled * scaled, axis=1)])
    parts = pair_total(parts, "core")
    parts = total(parts, "dp", 1)
    parts = pair_total(parts, "z")
    parts = total(parts, "z", 2)
    row_stats = DECAY * row_state + (1.0 - DECAY) * (parts[0] / F)
    here = jnp.sum(row_stats) / D
    inverse = lax.rsqrt(row_stats / here)
    power = jnp.sum(parts[1] * inverse * inverse)
    pair = jnp.stack([here, power])
    pairs = jnp.stack(direct(pair, "row"))
    row_mean = (pairs[0, 0] + pairs[2, 0]) + (pairs[1, 0] + pairs[3, 0])
    powers = pairs[:, 1] * (row_mean / pairs[:, 0])
    power_sum = (powers[0] + powers[2]) + (powers[1] + powers[3])
    clip_factor = jnp.maximum(1.0, jnp.sqrt(power_sum / (D * F)) / CLIP)
    row_scale = lax.rsqrt(row_stats / row_mean) / clip_factor
    return (grad * row_scale[:, None] * col_scale[None, :], row_stats, col_stats)


def solution(mesh):
    fine = Mesh(mesh.devices.reshape(4, 4, 8, 2), ("dp", "row", "z", "core"))
    return jax.shard_map(
        on_device,
        mesh=fine,
        in_specs=(
            P(("dp", "z", "core"), "row"),
            P("dp", ("z", "core")),
            P("row"),
            P(("z", "core", "dp")),
        ),
        out_specs=(P("row", ("z", "core", "dp")), P("row"), P(("z", "core", "dp"))),
        check_vma=False,
    )
```

```python
import jax
import jax.numpy as jnp
from jax import lax
from jax.experimental import pallas as pl
from jax.experimental.pallas import tpu as pltpu
from jax.sharding import Mesh, PartitionSpec as P

D = 12288
F = 49152
DECAY = 0.7
CLIP = 1.0
SIZE = {"dp": 4, "row": 4, "z": 8, "core": 2}
GROUPS = ((0, 3), (3, 5), (5, 7), (7, 8))


SMALL = pltpu.CompilerParams(vmem_limit_bytes=6 * 2**20)


def shift(x, axis, step):
    n = SIZE[axis]
    return lax.ppermute(x, axis, [(i, (i + step) % n) for i in range(n)])


def swap(x):
    return shift(x, "core", 1)


def apart(x, axis, step=1):
    n = SIZE[axis]
    pairs = [(2 * i + c, 2 * ((i + step * (1 - 2 * c)) % n) + c) for i in range(n) for c in (0, 1)]
    return lax.ppermute(x, (axis, "core"), pairs)


def direct(x, axis):
    return [x] + [shift(x, axis, s) for s in range(1, SIZE[axis])]


def flip(x, axis):
    return lax.ppermute(x, axis, [(i, i ^ 1) for i in range(SIZE[axis])])


def four(x, axis, step):
    one = apart(x, axis, step)
    return x, shift(x, axis, 2 * step), one, swap(one)


def grouped(x, axis, step):
    a, b, c, d = four(x, axis, step)
    return (a + b) + (c + d)


def total(x, axis, step):
    return (x + shift(x, axis, 2 * step)) + (shift(x, axis, step) + shift(x, axis, -step))


def order_kernel(place, own, near, far, out):
    z, core, row = place[0], place[1], place[2]
    sign = 2 * core - 1
    offsets = [0] + [o for s in (1, 2, 3) for o in (sign * s, -sign * s)] + [4]
    for slot, offset in enumerate(offsets):
        source = lax.rem(z + offset + 8, 8)
        here = lax.rem(lax.div(source, 4) + row, 2) == 0
        for c in (0, 1):
            inner = pl.multiple_of(lax.rem(source, 4) * 32 + c * 16, 16)
            outer = pl.multiple_of(source * 32 + c * 16, 16)
            base = (slot * 2 + c) * 64
            out[pl.ds(base, 16), :] = own[pl.ds(outer, 16), :]
            for dp in range(3):
                rows = pl.ds(inner, 16)
                value = jnp.where(here, near[dp, rows, :], far[dp, rows, :])
                out[pl.ds(base + (dp + 1) * 16, 16), :] = value


def order(place, own, near, far):
    return pl.pallas_call(
        order_kernel,
        out_shape=jax.ShapeDtypeStruct((1024, 768), jnp.bfloat16),
        in_specs=[pl.BlockSpec(memory_space=pltpu.SMEM)]
        + [pl.BlockSpec(memory_space=pltpu.VMEM)] * 3,
        out_specs=pl.BlockSpec(memory_space=pltpu.VMEM),
        compiler_params=SMALL,
    )(place, own, near, far)


def whole_sum(x):
    return jnp.sum(x, axis=(0, 1), keepdims=True)


def rows_kernel(p0, p1, p2, p3, state, stats, pair):
    parts = (p0[...] + p1[...]) + (p2[...] + p3[...])
    rows = DECAY * state[...] + (1.0 - DECAY) * (parts[:24] / F)
    here = whole_sum(rows) / D
    inverse = lax.rsqrt(rows / here)
    power = whole_sum(parts[24:] * inverse * inverse)
    stats[...] = rows
    pair[0:1, :] = jnp.broadcast_to(here, (1, 128))
    pair[1:2, :] = jnp.broadcast_to(power, (1, 128))


def rows_call(parts, state):
    return pl.pallas_call(
        rows_kernel,
        out_shape=[
            jax.ShapeDtypeStruct((24, 128), jnp.float32),
            jax.ShapeDtypeStruct((2, 128), jnp.float32),
        ],
        in_specs=[pl.BlockSpec(memory_space=pltpu.VMEM)] * 5,
        out_specs=[pl.BlockSpec(memory_space=pltpu.VMEM)] * 2,
        compiler_params=SMALL,
    )(*parts, state)


def update_kernel(p0, p1, p2, p3, stats, scale, grad0, grad1, out, buffer, sems):
    shares = [p[...] for p in (p0, p1, p2, p3)]
    row_mean = (shares[0][0:1] + shares[1][0:1]) + (shares[2][0:1] + shares[3][0:1])
    powers = [p[1:2] * (row_mean / p[0:1]) for p in shares]
    power_sum = (powers[0] + powers[1]) + (powers[2] + powers[3])
    clip_factor = jnp.maximum(1.0, jnp.sqrt(power_sum / (D * F)) / CLIP)
    row_scale = lax.rsqrt(stats[...] / row_mean) / clip_factor
    copies = [None] * 12
    for k in range(12):
        grad = (grad0, grad1)[k // 6]
        if k >= 4:
            copies[k - 4].wait()
        for j in range(2):
            row = row_scale[2 * k + j : 2 * k + j + 1, :]
            down = jnp.transpose(jnp.broadcast_to(row, (128, 128)))
            start = (k % 6) * 256 + j * 128
            for c in range(0, 768, 128):
                value = grad[start : start + 128, c : c + 128] * down
                buffer[k % 4, j * 128 : (j + 1) * 128, c : c + 128] = value * scale[:, c : c + 128]
        copies[k] = pltpu.make_async_copy(
            buffer.at[k % 4], out.at[pl.ds(k * 256, 256), :], sems.at[k % 4]
        )
        copies[k].start()
    for k in range(8, 12):
        copies[k].wait()


def update_call(shares, stats, scale, grads):
    return pl.pallas_call(
        update_kernel,
        out_shape=jax.ShapeDtypeStruct((3072, 768), jnp.float32),
        in_specs=[pl.BlockSpec(memory_space=pltpu.VMEM)] * 8,
        out_specs=pl.BlockSpec(memory_space=pl.ANY),
        scratch_shapes=[
            pltpu.VMEM((4, 256, 768), jnp.float32),
            pltpu.SemaphoreType.DMA((4,)),
        ],
        compiler_params=SMALL,
    )(*shares, stats, scale, *grads)


def on_device(tokens_in, out_grad, row_state, col_state):
    dp, row, z, core = (lax.axis_index(axis) for axis in SIZE)
    first = core == 0

    def by_core(own, other):
        return jnp.where(first, own, other), jnp.where(first, other, own)

    def tie(*values):
        return lax.optimization_barrier(values)

    own = jnp.concatenate(direct(tokens_in, "dp"), axis=0)
    whole = jnp.concatenate(by_core(own, swap(own)), axis=0)
    here = [whole[:, :1536], whole[:, 1536:]]
    halves = [[x] for x in here]

    def units(s, start, size):
        return lax.dynamic_slice(out_grad, (start, ((dp + s) % 4) * 768), (size, 768))

    near = jnp.stack([shift(units(s, row % 2 * 128, 128), "dp", s) for s in (1, 2, 3)])
    parcels = [units(0, 0, 256), near, flip(near, "row")]

    def ring_step(here):
        here = [apart(x, "z") for x in here]
        for half, x in zip(halves, here):
            half += [x, swap(x)]
        return here

    def product(h, lo, hi):
        tokens = jnp.concatenate(halves[h][lo:hi], axis=0)
        rows = b[lo * 128 : hi * 128]
        return lax.dot_general(
            tokens, rows, (((0,), (0,)), ((), ())), preferred_element_type=jnp.float32
        )

    here = ring_step(ring_step(here))
    here, parcels = tie(here, parcels)
    b = order(jnp.stack([z, core, row % 2]), *parcels)
    here = ring_step(here)
    grads = [product(h, 0, 3) for h in (0, 1)]
    here[1], grads = tie(here[1], grads)
    far = apart(by_core(*here)[0], "z")
    grads = [grads[h] + product(h, 3, 7) for h in (0, 1)]
    far, grads = tie(far, grads)
    for half, x in zip(halves, by_core(far, swap(far))):
        half.append(x)
    grads = [grads[h] + product(h, 7, 8) for h in (0, 1)]

    col_part = sum(jnp.sum(grad * grad, axis=0) for grad in grads)
    col_sum = total(col_part, "row", 1)
    col_stats = DECAY * col_state + (1.0 - DECAY) * (col_sum / D)
    col_scale = lax.rsqrt(col_stats)
    scaled = [grad * col_scale[None, :] for grad in grads]
    parts = [jnp.sum(x * x, axis=1).reshape(12, 128) for x in grads + scaled]
    parts = jnp.concatenate(parts, axis=0)
    parts = parts + swap(parts)
    parts = grouped(parts, "dp", 1)
    parts = parts + flip(parts, "z")
    row_stats, pair = rows_call(four(parts, "z", 2), row_state.reshape(24, 128))
    update = update_call(four(pair, "row", 1), row_stats, col_scale.reshape(1, 768), grads)
    return (update, row_stats.reshape(3072), col_stats)


def solution(mesh):
    fine = Mesh(mesh.devices.reshape(4, 4, 8, 2), ("dp", "row", "z", "core"))
    return jax.shard_map(
        on_device,
        mesh=fine,
        in_specs=(
            P(("dp", "z", "core"), "row"),
            P("dp", ("z", "core")),
            P("row"),
            P(("z", "core", "dp")),
        ),
        out_specs=(P("row", ("z", "core", "dp")), P("row"), P(("z", "core", "dp"))),
        check_vma=False,
    )
```

```python
import jax
import jax.numpy as jnp
from jax import lax
from jax.experimental import pallas as pl
from jax.experimental.pallas import tpu as pltpu
from jax.sharding import Mesh, PartitionSpec as P

D = 12288
F = 49152
DECAY = 0.7
CLIP = 1.0
SIZE = {"dp": 4, "row": 4, "z": 8, "core": 2}
GROUPS = ((0, 3), (3, 5), (5, 7), (7, 8))


SMALL = pltpu.CompilerParams(vmem_limit_bytes=6 * 2**20)


def shift(x, axis, step):
    n = SIZE[axis]
    return lax.ppermute(x, axis, [(i, (i + step) % n) for i in range(n)])


def swap(x):
    return shift(x, "core", 1)


def apart(x, axis, step=1):
    n = SIZE[axis]
    pairs = [(2 * i + c, 2 * ((i + step * (1 - 2 * c)) % n) + c) for i in range(n) for c in (0, 1)]
    return lax.ppermute(x, (axis, "core"), pairs)


def direct(x, axis):
    return [x] + [shift(x, axis, s) for s in range(1, SIZE[axis])]


def flip(x, axis):
    return lax.ppermute(x, axis, [(i, i ^ 1) for i in range(SIZE[axis])])


def four(x, axis, step):
    one = apart(x, axis, step)
    return x, shift(x, axis, 2 * step), one, swap(one)


def grouped(x, axis, step):
    a, b, c, d = four(x, axis, step)
    return (a + b) + (c + d)


def total(x, axis, step):
    return (x + shift(x, axis, 2 * step)) + (shift(x, axis, step) + shift(x, axis, -step))


def order_kernel(place, own, near, far, out):
    z, core, row = place[0], place[1], place[2]
    sign = 2 * core - 1
    offsets = [0] + [o for s in (1, 2, 3) for o in (sign * s, -sign * s)] + [4]
    for slot, offset in enumerate(offsets):
        source = lax.rem(z + offset + 8, 8)
        here = lax.rem(lax.div(source, 4) + row, 2) == 0
        for c in (0, 1):
            inner = pl.multiple_of(lax.rem(source, 4) * 32 + c * 16, 16)
            outer = pl.multiple_of(source * 32 + c * 16, 16)
            base = (slot * 2 + c) * 64
            out[pl.ds(base, 16), :] = own[pl.ds(outer, 16), :]
            for dp in range(3):
                rows = pl.ds(inner, 16)
                value = jnp.where(here, near[dp, rows, :], far[dp, rows, :])
                out[pl.ds(base + (dp + 1) * 16, 16), :] = value


def order(place, own, near, far):
    return pl.pallas_call(
        order_kernel,
        out_shape=jax.ShapeDtypeStruct((1024, 768), jnp.bfloat16),
        in_specs=[pl.BlockSpec(memory_space=pltpu.SMEM)]
        + [pl.BlockSpec(memory_space=pltpu.VMEM)] * 3,
        out_specs=pl.BlockSpec(memory_space=pltpu.VMEM),
        compiler_params=SMALL,
    )(place, own, near, far)


def whole_sum(x):
    return jnp.sum(x, axis=(0, 1), keepdims=True)


def rows_kernel(p0, p1, p2, p3, state, stats, same, pair):
    parts = (p0[...] + p1[...]) + (p2[...] + p3[...])
    rows = DECAY * state[...] + (1.0 - DECAY) * (parts[:24] / F)
    here = whole_sum(rows) / D
    inverse = lax.rsqrt(rows / here)
    power = whole_sum(parts[24:] * inverse * inverse)
    stats[...] = rows
    same[...] = rows
    pair[0:1, :] = jnp.broadcast_to(here, (1, 128))
    pair[1:2, :] = jnp.broadcast_to(power, (1, 128))


def rows_call(parts, state):
    return pl.pallas_call(
        rows_kernel,
        out_shape=[
            jax.ShapeDtypeStruct((24, 128), jnp.float32),
            jax.ShapeDtypeStruct((24, 128), jnp.float32),
            jax.ShapeDtypeStruct((2, 128), jnp.float32),
        ],
        in_specs=[pl.BlockSpec(memory_space=pltpu.VMEM)] * 5,
        out_specs=[pl.BlockSpec(memory_space=pltpu.VMEM)] * 3,
        compiler_params=SMALL,
    )(*parts, state)


def update_kernel(p0, p1, p2, p3, stats, scale, grad0, grad1, out, buffer, sems):
    shares = [p[...] for p in (p0, p1, p2, p3)]
    row_mean = (shares[0][0:1] + shares[1][0:1]) + (shares[2][0:1] + shares[3][0:1])
    powers = [p[1:2] * (row_mean / p[0:1]) for p in shares]
    power_sum = (powers[0] + powers[1]) + (powers[2] + powers[3])
    clip_factor = jnp.maximum(1.0, jnp.sqrt(power_sum / (D * F)) / CLIP)
    row_scale = lax.rsqrt(stats[...] / row_mean) / clip_factor
    copies = [None] * 12
    for k in range(12):
        grad = (grad0, grad1)[k // 6]
        if k >= 4:
            copies[k - 4].wait()
        for j in range(2):
            row = row_scale[2 * k + j : 2 * k + j + 1, :]
            down = jnp.transpose(jnp.broadcast_to(row, (128, 128)))
            start = (k % 6) * 256 + j * 128
            for c in range(0, 768, 128):
                value = grad[start : start + 128, c : c + 128] * down
                buffer[k % 4, j * 128 : (j + 1) * 128, c : c + 128] = value * scale[:, c : c + 128]
        copies[k] = pltpu.make_async_copy(
            buffer.at[k % 4], out.at[pl.ds(k * 256, 256), :], sems.at[k % 4]
        )
        copies[k].start()
    for k in range(8, 12):
        copies[k].wait()


def update_call(shares, stats, scale, grads):
    return pl.pallas_call(
        update_kernel,
        out_shape=jax.ShapeDtypeStruct((3072, 768), jnp.float32),
        in_specs=[pl.BlockSpec(memory_space=pltpu.VMEM)] * 8,
        out_specs=pl.BlockSpec(memory_space=pl.ANY),
        scratch_shapes=[
            pltpu.VMEM((4, 256, 768), jnp.float32),
            pltpu.SemaphoreType.DMA((4,)),
        ],
        compiler_params=SMALL,
    )(*shares, stats, scale, *grads)


def on_device(tokens_in, out_grad, row_state, col_state):
    dp, row, z, core = (lax.axis_index(axis) for axis in SIZE)
    first = core == 0

    def by_core(own, other):
        return jnp.where(first, own, other), jnp.where(first, other, own)

    def tie(*values):
        return lax.optimization_barrier(values)

    own = jnp.concatenate(direct(tokens_in, "dp"), axis=0)
    whole = jnp.concatenate(by_core(own, swap(own)), axis=0)
    here = [whole[:, :1536], whole[:, 1536:]]
    halves = [[x] for x in here]

    def units(s, start, size):
        return lax.dynamic_slice(out_grad, (start, ((dp + s) % 4) * 768), (size, 768))

    near = jnp.stack([shift(units(s, row % 2 * 128, 128), "dp", s) for s in (1, 2, 3)])
    parcels = [units(0, 0, 256), near, apart(near, "row")]

    def ring_step(here):
        here = [apart(x, "z") for x in here]
        for half, x in zip(halves, here):
            half += [x, swap(x)]
        return here

    def product(h, lo, hi):
        (tokens,) = tie(jnp.concatenate(halves[h][lo:hi], axis=0))
        rows = b[lo * 128 : hi * 128]
        return lax.dot_general(
            tokens, rows, (((0,), (0,)), ((), ())), preferred_element_type=jnp.float32
        )

    here = ring_step(ring_step(ring_step(here)))
    here[1], parcels = tie(here[1], parcels)
    far = apart(by_core(*here)[0], "z")
    b = order(jnp.stack([z, core, row % 2]), *parcels)
    grads = [product(h, 0, 3) for h in (0, 1)]
    grads = [grads[h] + product(h, 3, 7) for h in (0, 1)]
    far, grads = tie(far, grads)
    for half, x in zip(halves, by_core(far, swap(far))):
        half.append(x)
    (grads,) = tie([grads[h] + product(h, 7, 8) for h in (0, 1)])

    col_part = sum(jnp.sum(grad * grad, axis=0) for grad in grads)
    col_sum = total(col_part, "row", 1)
    col_stats = DECAY * col_state + (1.0 - DECAY) * (col_sum / D)
    col_scale = lax.rsqrt(col_stats)
    scaled = [grad * col_scale[None, :] for grad in grads]
    parts = [jnp.sum(x * x, axis=1).reshape(12, 128) for x in grads + scaled]
    parts = jnp.concatenate(parts, axis=0)
    parts = parts + swap(parts)
    parts = grouped(parts, "dp", 1)
    parts = parts + flip(parts, "z")
    row_stats, rows, pair = rows_call(four(parts, "z", 2), row_state.reshape(24, 128))
    update = update_call(four(pair, "row", 1), rows, col_scale.reshape(1, 768), grads)
    return (update, row_stats.reshape(3072), col_stats)


def solution(mesh):
    fine = Mesh(mesh.devices.reshape(4, 4, 8, 2), ("dp", "row", "z", "core"))
    return jax.shard_map(
        on_device,
        mesh=fine,
        in_specs=(
            P(("dp", "z", "core"), "row"),
            P("dp", ("z", "core")),
            P("row"),
            P(("z", "core", "dp")),
        ),
        out_specs=(P("row", ("z", "core", "dp")), P("row"), P(("z", "core", "dp"))),
        check_vma=False,
    )
```

```python
import jax
import jax.numpy as jnp
from jax import lax
from jax.experimental import pallas as pl
from jax.experimental.pallas import tpu as pltpu
from jax.sharding import Mesh, PartitionSpec as P

D = 12288
F = 49152
DECAY = 0.7
CLIP = 1.0
SIZE = {"dp": 4, "row": 4, "z": 8, "core": 2}
GROUPS = ((0, 3), (3, 5), (5, 7), (7, 8))


SMALL = pltpu.CompilerParams(vmem_limit_bytes=6 * 2**20)


def shift(x, axis, step):
    n = SIZE[axis]
    return lax.ppermute(x, axis, [(i, (i + step) % n) for i in range(n)])


def swap(x):
    return shift(x, "core", 1)


def apart(x, axis, step=1):
    n = SIZE[axis]
    pairs = [(2 * i + c, 2 * ((i + step * (1 - 2 * c)) % n) + c) for i in range(n) for c in (0, 1)]
    return lax.ppermute(x, (axis, "core"), pairs)


def direct(x, axis):
    return [x] + [shift(x, axis, s) for s in range(1, SIZE[axis])]


def flip(x, axis):
    return lax.ppermute(x, axis, [(i, i ^ 1) for i in range(SIZE[axis])])


def four(x, axis, step):
    one = apart(x, axis, step)
    return x, shift(x, axis, 2 * step), one, swap(one)


def grouped(x, axis, step):
    a, b, c, d = four(x, axis, step)
    return (a + b) + (c + d)


def total(x, axis, step):
    return (x + shift(x, axis, 2 * step)) + (shift(x, axis, step) + shift(x, axis, -step))


def order_kernel(place, own, near, far, out):
    z, core, row = place[0], place[1], place[2]
    sign = 2 * core - 1
    offsets = [0] + [o for s in (1, 2, 3) for o in (sign * s, -sign * s)] + [4]
    for slot, offset in enumerate(offsets):
        source = lax.rem(z + offset + 8, 8)
        here = lax.rem(lax.div(source, 4) + row, 2) == 0
        for c in (0, 1):
            inner = pl.multiple_of(lax.rem(source, 4) * 32 + c * 16, 16)
            outer = pl.multiple_of(source * 32 + c * 16, 16)
            base = (slot * 2 + c) * 64
            out[pl.ds(base, 16), :] = own[pl.ds(outer, 16), :]
            for dp in range(3):
                rows = pl.ds(inner, 16)
                value = jnp.where(here, near[dp, rows, :], far[dp, rows, :])
                out[pl.ds(base + (dp + 1) * 16, 16), :] = value


def order(place, own, near, far):
    return pl.pallas_call(
        order_kernel,
        out_shape=jax.ShapeDtypeStruct((1024, 768), jnp.bfloat16),
        in_specs=[pl.BlockSpec(memory_space=pltpu.SMEM)]
        + [pl.BlockSpec(memory_space=pltpu.VMEM)] * 3,
        out_specs=pl.BlockSpec(memory_space=pltpu.VMEM),
        compiler_params=SMALL,
    )(place, own, near, far)


def whole_sum(x):
    return jnp.sum(x, axis=(0, 1), keepdims=True)


def rows_kernel(p0, p1, p2, p3, state, stats, same, pair):
    parts = (p0[...] + p1[...]) + (p2[...] + p3[...])
    rows = DECAY * state[...] + (1.0 - DECAY) * (parts[:24] / F)
    here = whole_sum(rows) / D
    inverse = lax.rsqrt(rows / here)
    power = whole_sum(parts[24:] * inverse * inverse)
    stats[...] = rows
    same[...] = rows
    pair[0:1, :] = jnp.broadcast_to(here, (1, 128))
    pair[1:2, :] = jnp.broadcast_to(power, (1, 128))


def rows_call(parts, state):
    return pl.pallas_call(
        rows_kernel,
        out_shape=[
            jax.ShapeDtypeStruct((24, 128), jnp.float32),
            jax.ShapeDtypeStruct((24, 128), jnp.float32),
            jax.ShapeDtypeStruct((2, 128), jnp.float32),
        ],
        in_specs=[pl.BlockSpec(memory_space=pltpu.VMEM)] * 5,
        out_specs=[pl.BlockSpec(memory_space=pltpu.VMEM)] * 3,
        compiler_params=SMALL,
    )(*parts, state)


def update_kernel(core, p0, p1, p2, p3, stats, scale, grad0, grad1, out, scales, buffer, sems):
    shares = [p[...] for p in (p0, p1, p2, p3)]
    row_mean = (shares[0][0:1] + shares[1][0:1]) + (shares[2][0:1] + shares[3][0:1])
    powers = [p[1:2] * (row_mean / p[0:1]) for p in shares]
    power_sum = (powers[0] + powers[1]) + (powers[2] + powers[3])
    clip_factor = jnp.maximum(1.0, jnp.sqrt(power_sum / (D * F)) / CLIP)
    scales[...] = lax.rsqrt(stats[...] / row_mean) / clip_factor
    copies = [None] * 12
    for k in range(12):
        grad, half = ((grad0, core[0]), (grad1, 1 - core[0]))[k // 6]
        if k >= 4:
            copies[k - 4].wait()
        for j in range(2):
            row = scales[pl.ds(half * 12 + (k % 6) * 2 + j, 1), :]
            down = jnp.transpose(jnp.broadcast_to(row, (128, 128)))
            start = (k % 6) * 256 + j * 128
            for c in range(0, 768, 128):
                value = grad[start : start + 128, c : c + 128] * down
                buffer[k % 4, j * 128 : (j + 1) * 128, c : c + 128] = value * scale[:, c : c + 128]
        rows = pl.ds(pl.multiple_of(half * 1536 + (k % 6) * 256, 256), 256)
        copies[k] = pltpu.make_async_copy(buffer.at[k % 4], out.at[rows, :], sems.at[k % 4])
        copies[k].start()
    for k in range(8, 12):
        copies[k].wait()


def update_call(core, shares, stats, scale, grads):
    return pl.pallas_call(
        update_kernel,
        out_shape=jax.ShapeDtypeStruct((3072, 768), jnp.float32),
        in_specs=[pl.BlockSpec(memory_space=pltpu.SMEM)]
        + [pl.BlockSpec(memory_space=pltpu.VMEM)] * 8,
        out_specs=pl.BlockSpec(memory_space=pl.ANY),
        scratch_shapes=[
            pltpu.VMEM((24, 128), jnp.float32),
            pltpu.VMEM((4, 256, 768), jnp.float32),
            pltpu.SemaphoreType.DMA((4,)),
        ],
        compiler_params=SMALL,
    )(core.reshape(1), *shares, stats, scale, *grads)


def on_device(tokens_in, out_grad, row_state, col_state):
    dp, row, z, core = (lax.axis_index(axis) for axis in SIZE)
    first = core == 0

    def by_core(own, other):
        return jnp.where(first, own, other), jnp.where(first, other, own)

    def tie(*values):
        return lax.optimization_barrier(values)

    own = jnp.concatenate(direct(tokens_in, "dp"), axis=0)
    whole = jnp.concatenate(by_core(own, swap(own)), axis=0)
    here = list(by_core(whole[:, :1536], whole[:, 1536:]))
    halves = [[x] for x in here]

    def units(s, start, size):
        return lax.dynamic_slice(out_grad, (start, ((dp + s) % 4) * 768), (size, 768))

    near = jnp.stack([shift(units(s, row % 2 * 128, 128), "dp", s) for s in (1, 2, 3)])
    parcels = [units(0, 0, 256), near, apart(near, "row")]

    def ring_step(here):
        here = [apart(x, "z") for x in here]
        halves[0] += [here[0], swap(here[1])]
        halves[1] += [here[1], swap(here[0])]
        return here

    def product(h, lo, hi):
        (tokens,) = tie(jnp.concatenate(halves[h][lo:hi], axis=0))
        rows = b[lo * 128 : hi * 128]
        return lax.dot_general(
            tokens, rows, (((0,), (0,)), ((), ())), preferred_element_type=jnp.float32
        )

    here = ring_step(ring_step(ring_step(here)))
    here[0], parcels = tie(here[0], parcels)
    far = apart(here[0], "z")
    b = order(jnp.stack([z, core, row % 2]), *parcels)
    grads = [product(h, 0, 3) for h in (0, 1)]
    grads = [grads[h] + product(h, 3, 7) for h in (0, 1)]
    far, grads[0] = tie(far, grads[0])
    halves[0].append(far)
    halves[1].append(swap(far))
    (grads,) = tie([grads[h] + product(h, 7, 8) for h in (0, 1)])

    col_part = sum(jnp.sum(grad * grad, axis=0) for grad in grads)
    col_sum = total(col_part, "row", 1)
    col_stats = DECAY * col_state + (1.0 - DECAY) * (col_sum / D)
    col_scale = lax.rsqrt(col_stats)
    scaled = [grad * col_scale[None, :] for grad in grads]
    parts = [jnp.sum(x * x, axis=1).reshape(12, 128) for x in grads + scaled]
    parts = jnp.concatenate([*by_core(*parts[:2]), *by_core(*parts[2:])], axis=0)
    parts = parts + swap(parts)
    parts = grouped(parts, "dp", 1)
    parts = parts + flip(parts, "z")
    row_stats, rows, pair = rows_call(four(parts, "z", 2), row_state.reshape(24, 128))
    update = update_call(core, four(pair, "row", 1), rows, col_scale.reshape(1, 768), grads)
    return (update, row_stats.reshape(3072), col_stats)


def solution(mesh):
    fine = Mesh(mesh.devices.reshape(4, 4, 8, 2), ("dp", "row", "z", "core"))
    return jax.shard_map(
        on_device,
        mesh=fine,
        in_specs=(
            P(("dp", "z", "core"), "row"),
            P("dp", ("z", "core")),
            P("row"),
            P(("z", "core", "dp")),
        ),
        out_specs=(P("row", ("z", "core", "dp")), P("row"), P(("z", "core", "dp"))),
        check_vma=False,
    )
```

```python
import jax
import jax.numpy as jnp
from jax import lax
from jax.experimental import pallas as pl
from jax.experimental.pallas import tpu as pltpu
from jax.sharding import Mesh, PartitionSpec as P

D = 12288
F = 49152
DECAY = 0.7
CLIP = 1.0
SIZE = {"dp": 4, "row": 4, "z": 8, "core": 2}


SMALL = pltpu.CompilerParams(vmem_limit_bytes=6 * 2**20)


def shift(x, axis, step):
    n = SIZE[axis]
    return lax.ppermute(x, axis, [(i, (i + step) % n) for i in range(n)])


def swap(x):
    return shift(x, "core", 1)


def apart(x, axis, step=1):
    n = SIZE[axis]
    pairs = [(2 * i + c, 2 * ((i + step * (1 - 2 * c)) % n) + c) for i in range(n) for c in (0, 1)]
    return lax.ppermute(x, (axis, "core"), pairs)


def direct(x, axis):
    return [x] + [shift(x, axis, s) for s in range(1, SIZE[axis])]


def flip(x, axis):
    return lax.ppermute(x, axis, [(i, i ^ 1) for i in range(SIZE[axis])])


def four(x, axis, step):
    one = apart(x, axis, step)
    return x, shift(x, axis, 2 * step), one, swap(one)


def grouped(x, axis, step):
    a, b, c, d = four(x, axis, step)
    return (a + b) + (c + d)


def total(x, axis, step):
    return (x + shift(x, axis, 2 * step)) + (shift(x, axis, step) + shift(x, axis, -step))


def order_kernel(place, own, near, far, out):
    z, core, row = place[0], place[1], place[2]
    sign = 2 * core - 1
    offsets = [0] + [o for s in (1, 2, 3) for o in (sign * s, -sign * s)] + [4]
    for slot, offset in enumerate(offsets):
        source = lax.rem(z + offset + 8, 8)
        here = lax.rem(lax.div(source, 4) + row, 2) == 0
        for c in (0, 1):
            inner = pl.multiple_of(lax.rem(source, 4) * 32 + c * 16, 16)
            outer = pl.multiple_of(source * 32 + c * 16, 16)
            base = (slot * 2 + c) * 64
            out[pl.ds(base, 16), :] = own[pl.ds(outer, 16), :]
            for dp in range(3):
                rows = pl.ds(inner, 16)
                value = jnp.where(here, near[dp, rows, :], far[dp, rows, :])
                out[pl.ds(base + (dp + 1) * 16, 16), :] = value


def order(place, own, near, far):
    return pl.pallas_call(
        order_kernel,
        out_shape=jax.ShapeDtypeStruct((1024, 768), jnp.bfloat16),
        in_specs=[pl.BlockSpec(memory_space=pltpu.SMEM)]
        + [pl.BlockSpec(memory_space=pltpu.VMEM)] * 3,
        out_specs=pl.BlockSpec(memory_space=pltpu.VMEM),
        compiler_params=SMALL,
    )(place, own, near, far)


def whole_sum(x):
    return jnp.sum(x, axis=(0, 1), keepdims=True)


def rows_kernel(p0, p1, p2, p3, state, stats, same, pair):
    parts = (p0[...] + p1[...]) + (p2[...] + p3[...])
    rows = DECAY * state[...] + (1.0 - DECAY) * (parts[:24] / F)
    here = whole_sum(rows) / D
    inverse = lax.rsqrt(rows / here)
    power = whole_sum(parts[24:] * inverse * inverse)
    stats[...] = rows
    same[...] = rows
    pair[0:1, :] = jnp.broadcast_to(here, (1, 128))
    pair[1:2, :] = jnp.broadcast_to(power, (1, 128))


def rows_call(parts, state):
    return pl.pallas_call(
        rows_kernel,
        out_shape=[
            jax.ShapeDtypeStruct((24, 128), jnp.float32),
            jax.ShapeDtypeStruct((24, 128), jnp.float32),
            jax.ShapeDtypeStruct((2, 128), jnp.float32),
        ],
        in_specs=[pl.BlockSpec(memory_space=pltpu.VMEM)] * 5,
        out_specs=[pl.BlockSpec(memory_space=pltpu.VMEM)] * 3,
        compiler_params=SMALL,
    )(*parts, state)


def update_kernel(core, p0, p1, p2, p3, stats, scale, grad0, grad1, out, scales, buffer, sems):
    shares = [p[...] for p in (p0, p1, p2, p3)]
    row_mean = (shares[0][0:1] + shares[1][0:1]) + (shares[2][0:1] + shares[3][0:1])
    powers = [p[1:2] * (row_mean / p[0:1]) for p in shares]
    power_sum = (powers[0] + powers[1]) + (powers[2] + powers[3])
    clip_factor = jnp.maximum(1.0, jnp.sqrt(power_sum / (D * F)) / CLIP)
    scales[...] = lax.rsqrt(stats[...] / row_mean) / clip_factor
    copies = [None] * 12
    for k in range(12):
        grad, half = ((grad0, core[0]), (grad1, 1 - core[0]))[k // 6]
        if k >= 4:
            copies[k - 4].wait()
        for j in range(2):
            row = scales[pl.ds(half * 12 + (k % 6) * 2 + j, 1), :]
            down = jnp.transpose(jnp.broadcast_to(row, (128, 128)))
            start = (k % 6) * 256 + j * 128
            for c in range(0, 768, 128):
                value = grad[start : start + 128, c : c + 128] * down
                buffer[k % 4, j * 128 : (j + 1) * 128, c : c + 128] = value * scale[:, c : c + 128]
        rows = pl.ds(pl.multiple_of(half * 1536 + (k % 6) * 256, 256), 256)
        copies[k] = pltpu.make_async_copy(buffer.at[k % 4], out.at[rows, :], sems.at[k % 4])
        copies[k].start()
    for k in range(8, 12):
        copies[k].wait()


def update_call(core, shares, stats, scale, grads):
    return pl.pallas_call(
        update_kernel,
        out_shape=jax.ShapeDtypeStruct((3072, 768), jnp.float32),
        in_specs=[pl.BlockSpec(memory_space=pltpu.SMEM)]
        + [pl.BlockSpec(memory_space=pltpu.VMEM)] * 8,
        out_specs=pl.BlockSpec(memory_space=pl.ANY),
        scratch_shapes=[
            pltpu.VMEM((24, 128), jnp.float32),
            pltpu.VMEM((4, 256, 768), jnp.float32),
            pltpu.SemaphoreType.DMA((4,)),
        ],
        compiler_params=SMALL,
    )(core.reshape(1), *shares, stats, scale, *grads)


def on_device(tokens_in, out_grad, row_state, col_state):
    dp, row, z, core = (lax.axis_index(axis) for axis in SIZE)
    first = core == 0

    def by_core(own, other):
        return jnp.where(first, own, other), jnp.where(first, other, own)

    def tie(*values):
        return lax.optimization_barrier(values)

    own = jnp.concatenate(direct(tokens_in, "dp"), axis=0)
    whole = jnp.concatenate(by_core(own, swap(own)), axis=0)
    here = list(by_core(whole[:, :1536], whole[:, 1536:]))
    halves = [[x] for x in here]

    def units(s, start, size):
        return lax.dynamic_slice(out_grad, (start, ((dp + s) % 4) * 768), (size, 768))

    near = jnp.stack([shift(units(s, row % 2 * 128, 128), "dp", s) for s in (1, 2, 3)])
    parcels = [units(0, 0, 256), near, apart(near, "row")]

    def ring_step(here):
        here = [apart(x, "z") for x in here]
        halves[0] += [here[0], swap(here[1])]
        halves[1] += [here[1], swap(here[0])]
        return here

    def product(tokens, rows):
        return lax.dot_general(
            tokens, rows, (((0,), (0,)), ((), ())), preferred_element_type=jnp.float32
        )

    here = ring_step(ring_step(ring_step(here)))
    here[0], parcels = tie(here[0], parcels)
    far = apart(here[0], "z")
    b = order(jnp.stack([z, core, row % 2]), *parcels)
    blank = jnp.zeros((128, 1536), jnp.bfloat16)
    early, late = (
        [jnp.concatenate((half + [blank])[i : i + 4], axis=0) for half in halves] for i in (0, 4)
    )
    (early,) = tie(early)
    grads = [product(x, b[:512]) for x in early]
    far, grads, late = tie(far, grads, late)
    for h, x in enumerate((far, swap(far))):
        (tokens,) = tie(lax.dynamic_update_slice(late[h], x, (384, 0)))
        (grads[h],) = tie(grads[h] + product(tokens, b[512:]))

    col_part = sum(jnp.sum(grad * grad, axis=0) for grad in grads)
    col_sum = total(col_part, "row", 1)
    col_stats = DECAY * col_state + (1.0 - DECAY) * (col_sum / D)
    col_scale = lax.rsqrt(col_stats)
    scaled = [grad * col_scale[None, :] for grad in grads]
    parts = [jnp.sum(x * x, axis=1).reshape(12, 128) for x in grads + scaled]
    parts = jnp.concatenate([*by_core(*parts[:2]), *by_core(*parts[2:])], axis=0)
    parts = parts + swap(parts)
    parts = grouped(parts, "dp", 1)
    parts = parts + flip(parts, "z")
    row_stats, rows, pair = rows_call(four(parts, "z", 2), row_state.reshape(24, 128))
    update = update_call(core, four(pair, "row", 1), rows, col_scale.reshape(1, 768), grads)
    return (update, row_stats.reshape(3072), col_stats)


def solution(mesh):
    fine = Mesh(mesh.devices.reshape(4, 4, 8, 2), ("dp", "row", "z", "core"))
    return jax.shard_map(
        on_device,
        mesh=fine,
        in_specs=(
            P(("dp", "z", "core"), "row"),
            P("dp", ("z", "core")),
            P("row"),
            P(("z", "core", "dp")),
        ),
        out_specs=(P("row", ("z", "core", "dp")), P("row"), P(("z", "core", "dp"))),
        check_vma=False,
    )
```

```python
import jax
import jax.numpy as jnp
from jax import lax
from jax.experimental import pallas as pl
from jax.experimental.pallas import tpu as pltpu
from jax.sharding import Mesh, PartitionSpec as P

D = 12288
F = 49152
DECAY = 0.7
CLIP = 1.0
SIZE = {"dp": 4, "row": 4, "z": 8, "core": 2}


SMALL = pltpu.CompilerParams(vmem_limit_bytes=6 * 2**20)


def shift(x, axis, step):
    n = SIZE[axis]
    return lax.ppermute(x, axis, [(i, (i + step) % n) for i in range(n)])


def swap(x):
    return shift(x, "core", 1)


def apart(x, axis, step=1):
    n = SIZE[axis]
    pairs = [(2 * i + c, 2 * ((i + step * (1 - 2 * c)) % n) + c) for i in range(n) for c in (0, 1)]
    return lax.ppermute(x, (axis, "core"), pairs)


def direct(x, axis):
    return [x] + [shift(x, axis, s) for s in range(1, SIZE[axis])]


def four(x, axis, step):
    one = apart(x, axis, step)
    return x, shift(x, axis, 2 * step), one, swap(one)


def grouped(x, axis, step):
    a, b, c, d = four(x, axis, step)
    return (a + b) + (c + d)


def total(x, axis, step):
    return (x + shift(x, axis, 2 * step)) + (shift(x, axis, step) + shift(x, axis, -step))


def order_kernel(place, own, near, far, out):
    z, core, row = place[0], place[1], place[2]
    sign = 2 * core - 1
    offsets = [0] + [o for s in (1, 2, 3) for o in (sign * s, -sign * s)] + [4]
    for slot, offset in enumerate(offsets):
        source = lax.rem(z + offset + 8, 8)
        here = lax.rem(lax.div(source, 4) + row, 2) == 0
        for c in (0, 1):
            inner = pl.multiple_of(lax.rem(source, 4) * 32 + c * 16, 16)
            outer = pl.multiple_of(source * 32 + c * 16, 16)
            base = (slot * 2 + c) * 64
            out[pl.ds(base, 16), :] = own[pl.ds(outer, 16), :]
            for dp in range(3):
                rows = pl.ds(inner, 16)
                value = jnp.where(here, near[dp, rows, :], far[dp, rows, :])
                out[pl.ds(base + (dp + 1) * 16, 16), :] = value


def order(place, own, near, far):
    return pl.pallas_call(
        order_kernel,
        out_shape=jax.ShapeDtypeStruct((1024, 768), jnp.bfloat16),
        in_specs=[pl.BlockSpec(memory_space=pltpu.SMEM)]
        + [pl.BlockSpec(memory_space=pltpu.VMEM)] * 3,
        out_specs=pl.BlockSpec(memory_space=pltpu.VMEM),
        compiler_params=SMALL,
    )(place, own, near, far)


def whole_sum(x):
    return jnp.sum(x, axis=(0, 1), keepdims=True)


def rows_kernel(p0, p4, a1, a2, a3, o1, o2, o3, state, stats, same, pair):
    even = (p0[...] + p4[...]) + (a2[...] + o2[...])
    odd = (a1[...] + o3[...]) + (o1[...] + a3[...])
    parts = even + odd
    rows = DECAY * state[...] + (1.0 - DECAY) * (parts[:24] / F)
    here = whole_sum(rows) / D
    inverse = lax.rsqrt(rows / here)
    power = whole_sum(parts[24:] * inverse * inverse)
    stats[...] = rows
    same[...] = rows
    pair[0:1, :] = jnp.broadcast_to(here, (1, 128))
    pair[1:2, :] = jnp.broadcast_to(power, (1, 128))


def rows_call(parts, state):
    return pl.pallas_call(
        rows_kernel,
        out_shape=[
            jax.ShapeDtypeStruct((24, 128), jnp.float32),
            jax.ShapeDtypeStruct((24, 128), jnp.float32),
            jax.ShapeDtypeStruct((2, 128), jnp.float32),
        ],
        in_specs=[pl.BlockSpec(memory_space=pltpu.VMEM)] * 9,
        out_specs=[pl.BlockSpec(memory_space=pltpu.VMEM)] * 3,
        compiler_params=SMALL,
    )(*parts, state)


def update_kernel(core, p0, p1, p2, p3, stats, scale, grad0, grad1, out, scales, buffer, sems):
    shares = [p[...] for p in (p0, p1, p2, p3)]
    row_mean = (shares[0][0:1] + shares[1][0:1]) + (shares[2][0:1] + shares[3][0:1])
    powers = [p[1:2] * (row_mean / p[0:1]) for p in shares]
    power_sum = (powers[0] + powers[1]) + (powers[2] + powers[3])
    clip_factor = jnp.maximum(1.0, jnp.sqrt(power_sum / (D * F)) / CLIP)
    scales[...] = lax.rsqrt(stats[...] / row_mean) / clip_factor
    copies = [None] * 12
    for k in range(12):
        grad, half = ((grad0, core[0]), (grad1, 1 - core[0]))[k // 6]
        if k >= 4:
            copies[k - 4].wait()
        for j in range(2):
            row = scales[pl.ds(half * 12 + (k % 6) * 2 + j, 1), :]
            down = jnp.transpose(jnp.broadcast_to(row, (128, 128)))
            start = (k % 6) * 256 + j * 128
            for c in range(0, 768, 128):
                value = grad[start : start + 128, c : c + 128] * down
                buffer[k % 4, j * 128 : (j + 1) * 128, c : c + 128] = value * scale[:, c : c + 128]
        rows = pl.ds(pl.multiple_of(half * 1536 + (k % 6) * 256, 256), 256)
        copies[k] = pltpu.make_async_copy(buffer.at[k % 4], out.at[rows, :], sems.at[k % 4])
        copies[k].start()
    for k in range(8, 12):
        copies[k].wait()


def update_call(core, shares, stats, scale, grads):
    return pl.pallas_call(
        update_kernel,
        out_shape=jax.ShapeDtypeStruct((3072, 768), jnp.float32),
        in_specs=[pl.BlockSpec(memory_space=pltpu.SMEM)]
        + [pl.BlockSpec(memory_space=pltpu.VMEM)] * 8,
        out_specs=pl.BlockSpec(memory_space=pl.ANY),
        scratch_shapes=[
            pltpu.VMEM((24, 128), jnp.float32),
            pltpu.VMEM((4, 256, 768), jnp.float32),
            pltpu.SemaphoreType.DMA((4,)),
        ],
        compiler_params=SMALL,
    )(core.reshape(1), *shares, stats, scale, *grads)


def on_device(tokens_in, out_grad, row_state, col_state):
    dp, row, z, core = (lax.axis_index(axis) for axis in SIZE)
    first = core == 0

    def by_core(own, other):
        return jnp.where(first, own, other), jnp.where(first, other, own)

    def tie(*values):
        return lax.optimization_barrier(values)

    own = jnp.concatenate(direct(tokens_in, "dp"), axis=0)
    whole = jnp.concatenate(by_core(own, swap(own)), axis=0)
    here = list(by_core(whole[:, :1536], whole[:, 1536:]))
    halves = [[x] for x in here]

    def units(s, start, size):
        return lax.dynamic_slice(out_grad, (start, ((dp + s) % 4) * 768), (size, 768))

    near = jnp.stack([shift(units(s, row % 2 * 128, 128), "dp", s) for s in (1, 2, 3)])
    parcels = [units(0, 0, 256), near, apart(near, "row")]

    def ring_step(here):
        here = [apart(x, "z") for x in here]
        halves[0] += [here[0], swap(here[1])]
        halves[1] += [here[1], swap(here[0])]
        return here

    def product(tokens, rows):
        return lax.dot_general(
            tokens, rows, (((0,), (0,)), ((), ())), preferred_element_type=jnp.float32
        )

    here = ring_step(ring_step(ring_step(here)))
    here[0], parcels = tie(here[0], parcels)
    far = apart(here[0], "z")
    b = order(jnp.stack([z, core, row % 2]), *parcels)
    blank = jnp.zeros((128, 1536), jnp.bfloat16)
    early, late = (
        [jnp.concatenate((half + [blank])[i : i + 4], axis=0) for half in halves] for i in (0, 4)
    )
    (early,) = tie(early)
    grads = [product(x, b[:512]) for x in early]
    far, grads, late = tie(far, grads, late)
    for h, x in enumerate((far, swap(far))):
        (tokens,) = tie(lax.dynamic_update_slice(late[h], x, (384, 0)))
        (grads[h],) = tie(grads[h] + product(tokens, b[512:]))

    col_part = sum(jnp.sum(grad * grad, axis=0) for grad in grads)
    col_sum = total(col_part, "row", 1)
    col_stats = DECAY * col_state + (1.0 - DECAY) * (col_sum / D)
    col_scale = lax.rsqrt(col_stats)
    scaled = [grad * col_scale[None, :] for grad in grads]
    parts = [jnp.sum(x * x, axis=1).reshape(12, 128) for x in grads + scaled]
    parts = jnp.concatenate([*by_core(*parts[:2]), *by_core(*parts[2:])], axis=0)
    parts = parts + swap(parts)
    parts = grouped(parts, "dp", 1)
    sides = [apart(parts, "z", step) for step in (1, 2, 3)]
    eight = [parts, shift(parts, "z", 4), *sides, *(swap(x) for x in sides)]
    row_stats, rows, pair = rows_call(eight, row_state.reshape(24, 128))
    update = update_call(core, four(pair, "row", 1), rows, col_scale.reshape(1, 768), grads)
    return (update, row_stats.reshape(3072), col_stats)


def solution(mesh):
    fine = Mesh(mesh.devices.reshape(4, 4, 8, 2), ("dp", "row", "z", "core"))
    return jax.shard_map(
        on_device,
        mesh=fine,
        in_specs=(
            P(("dp", "z", "core"), "row"),
            P("dp", ("z", "core")),
            P("row"),
            P(("z", "core", "dp")),
        ),
        out_specs=(P("row", ("z", "core", "dp")), P("row"), P(("z", "core", "dp"))),
        check_vma=False,
    )
```
